256 devices in a mesh: seq: 32 (over x, z_hi, core), batch: 8 (over z_lo, y).
Axes of the slice: x: 4, y: 4, z: 8 (z_hi: 4, z_lo: 2; z = z_hi * 2 + z_lo), core: 2. Of those that a mesh axis runs over, the one named last changes fastest.
Arguments:
- activations: bfloat16 [8, 16384, 1536], P('batch', 'seq'), may hold values from -60 to 60
- cotangent: bfloat16 [8, 16384, 1536], P('batch', 'seq'), may hold values from -6 to 6
- contig_lengths: int32 [8, 4], P('batch'), may hold values from 1 to 8192, 16384 in all within a row
- gain_input: float32 [1536], replicated, may hold values from 0.1 to 1.9
- tap_weights: bfloat16 [3, 1536, 768], replicated, may hold values from -0.09375 to 0.09375
- gain_middle: float32 [768], replicated, may hold values from 0.1 to 1.9
- point_weights: bfloat16 [768, 1536], replicated, may hold values from -0.21875 to 0.21875
Outputs:
- block_output: bfloat16 [8, 16384, 1536], P('batch', 'seq')
- input_grad: bfloat16 [8, 16384, 1536], P('batch', 'seq')
- gain_input_grad: float32 [1536], replicated
- gain_middle_grad: float32 [768], replicated
The draws below stay inside these ranges and needn't reach their ends.
Inputs may be any that keep to these rules, and one draw needn't show every extreme that they name: `contig_lengths`: row w lists in order the lengths of the 4 contigs packed into window w; they sum to 16384.
All inputs are finite; a program needn't handle non-finite values.
Results may differ from the reference program's by a relative error of at most 0.0065.
Values may be sent and summed in bfloat16 or wider, within the bound.
A program may use at most 64 MiB of HBM per device.

```python
import math
import jax
import jax.numpy as jnp
import numpy as np
from jax import lax

C = 1536
F = 768
ROWS_DEV = 512
SPAN = 2
NCONTIG = 4
LENGTH = 16384
WINDOWS = 8


def draw_activations(key, part):
    full_shape = (WINDOWS, LENGTH, C)
    key_values, key_rows, key_columns = jax.random.split(key, 3)
    lowest = math.log(0.3)
    highest = math.log(3.0)
    row_scale = jnp.exp(jax.random.uniform(key_rows, (WINDOWS, LENGTH, 1), jnp.float32, lowest, highest))
    column_scale = jnp.exp(jax.random.uniform(key_columns, (1, 1, C), jnp.float32, lowest, highest))
    values = jnp.clip(jax.random.normal(key_values, full_shape, jnp.float32), -6.0, 6.0)
    return (values * row_scale * column_scale).astype(jnp.bfloat16)


def shard_levels(own_key, extent, cuts, smallest, high):
    loudness = 1.0
    for axis_at, blocks in cuts:
        draws = jax.random.uniform(jax.random.fold_in(jax.random.fold_in(own_key, 6), axis_at), (blocks,), jnp.float32, smallest / len(cuts), high / len(cuts))
        loudness = loudness * jnp.repeat(jnp.exp(draws), extent[axis_at] // blocks).reshape((-1,) + (1,) * (len(extent) - 1 - axis_at))
    return loudness


def split_up(amount, total, most, slope):
    loads = [(1 << 20) // math.isqrt(rank ** slope) + 1 for rank in range(2, amount + 1)]
    spare, holding = total - most - (amount - 1), [1] * (amount - 1)
    while spare > 0:
        movable = [i for i in range(amount - 1) if holding[i] < most]
        whole, budget = sum([loads[i] for i in movable]), spare
        for i in movable:
            more = min(most - holding[i], max(1, budget * loads[i] // whole), spare)
            holding[i] = holding[i] + more
            spare = spare - more
    return np.array([most] + holding)


def uneven(key, number_of, total, bound, lean):
    if number_of == 2:
        one = jax.random.randint(key, (), max(1, total - bound), min(bound, total - 1) + 1)
        return jnp.stack([one, total - one])
    sizes = jnp.asarray(split_up(number_of, total, bound, lean), jnp.int32)
    couples = (number_of - 1) // 2
    source_of, receiver = sizes[1:1 + 2 * couples:2], sizes[2:2 + 2 * couples:2]
    room = jnp.minimum(source_of - 1, bound - receiver)
    moved = jax.random.randint(jax.random.fold_in(key, 1), (couples,), 0, 1 << 20) % (room + 1)
    sizes = sizes.at[1:1 + 2 * couples:2].set(source_of - moved).at[2:2 + 2 * couples:2].set(receiver + moved)
    return sizes[jax.random.permutation(jax.random.fold_in(key, 2), number_of)]


def centred(rng, shape, scale, limit, shards=(), kind=jnp.bfloat16):
    gain = shard_levels(rng, shape, shards, -0.22, 0.18) if shards else 1.0
    values = jax.random.normal(rng, shape, jnp.float32) * scale * gain
    return jnp.minimum(jnp.maximum(values, -limit), limit).astype(kind)


def setup_inputs(seed: int = 0) -> dict:
    key_list = jax.random.split(jax.random.key(seed), 8)
    return {
        "activations": draw_activations(jax.random.fold_in(key_list[7], 71), 0),
        "cotangent": centred(key_list[1], (WINDOWS, LENGTH, C), 1.0, 6.0, ((0, 8), (1, 32))),
        "contig_lengths": jax.vmap(lambda own: uneven(own, NCONTIG, LENGTH, LENGTH // 2, 2))(jax.random.split(key_list[2], WINDOWS)).reshape((WINDOWS, NCONTIG)).astype(jnp.int32),
        "gain_input": jnp.clip(1.0 + 0.18 * jax.random.normal(key_list[3], (C,), jnp.float32), 0.1, 1.9),
        "tap_weights": centred(key_list[4], (3, C, F), (3 * C) ** -0.5, 0.09375),
        "gain_middle": jnp.clip(1.0 + 0.18 * jax.random.normal(key_list[5], (F,), jnp.float32), 0.1, 1.9),
        "point_weights": centred(key_list[6], (F, C), F ** -0.5, 0.21875),
    }


epsilon = 1e-06

def norm_activate(values, scales):
    mean_square = lax.optimization_barrier(jnp.mean(values * values, axis=-1, keepdims=True))
    return jax.nn.gelu(values * lax.rsqrt(mean_square + epsilon) * scales, approximate=True)

def contig_owner(lengths, positions):
    bounds = jnp.cumsum(lengths).astype(jnp.int32)
    return lax.optimization_barrier(jnp.sum((positions[:, None] >= bounds[None, :]).astype(jnp.int32), axis=1)).astype(jnp.int32)

def shifted(values, offset):
    padding = jnp.zeros((abs(offset),) + values.shape[1:], values.dtype)
    if offset > 0:
        return jnp.concatenate([values[offset:], padding], axis=0)
    return jnp.concatenate([padding, values[:offset]], axis=0)

def reference(activations, cotangent, contig_lengths, gain_input, tap_weights, gain_middle, point_weights):
    tap_reach = SPAN * ROWS_DEV
    positions = jnp.arange(LENGTH, dtype=jnp.int32)
    tap_before = tap_weights[0]
    tap_center = tap_weights[1]
    tap_after = tap_weights[2]

    def window(inputs):
        signal, upstream, lengths = inputs
        owners = contig_owner(lengths, positions)
        before_valid = ((positions >= tap_reach) & (shifted(owners, -tap_reach) == owners)).astype(jnp.float32)[:, None]
        after_valid = ((positions < LENGTH - tap_reach) & (shifted(owners, tap_reach) == owners)).astype(jnp.float32)[:, None]
        normed, input_vjp = jax.vjp(norm_activate, signal.astype(jnp.float32), gain_input)
        hidden = normed.astype(jnp.bfloat16)
        combined = jnp.dot(hidden, tap_center, preferred_element_type=jnp.float32)
        combined = combined + before_valid * jnp.dot(shifted(hidden, -tap_reach), tap_before, preferred_element_type=jnp.float32)
        combined = combined + after_valid * jnp.dot(shifted(hidden, tap_reach), tap_after, preferred_element_type=jnp.float32)
        middle_f, middle_vjp = jax.vjp(norm_activate, combined, gain_middle)
        middle = middle_f.astype(jnp.bfloat16)
        output = (signal.astype(jnp.float32) + jnp.dot(middle, point_weights, preferred_element_type=jnp.float32)).astype(jnp.bfloat16)
        grad_middle = jnp.dot(upstream, point_weights.T, preferred_element_type=jnp.float32)
        grad_combined_f, middle_terms = middle_vjp(grad_middle)
        grad_combined = grad_combined_f.astype(jnp.bfloat16)
        grad_hidden = jnp.dot(grad_combined, tap_center.T, preferred_element_type=jnp.float32)
        grad_hidden = grad_hidden + before_valid * jnp.dot(shifted(grad_combined, -tap_reach), tap_after.T, preferred_element_type=jnp.float32)
        grad_hidden = grad_hidden + after_valid * jnp.dot(shifted(grad_combined, tap_reach), tap_before.T, preferred_element_type=jnp.float32)
        grad_signal, input_terms = input_vjp(grad_hidden)
        grad_output = (upstream.astype(jnp.float32) + grad_signal).astype(jnp.bfloat16)
        return (output, grad_output, input_terms, middle_terms)
    outputs, grads, input_terms, middle_terms = lax.map(window, (activations, cotangent, contig_lengths))
    factor = 1.0 / (WINDOWS * LENGTH) ** 0.5
    return (outputs, grads, lax.optimization_barrier(jnp.sum(input_terms, axis=0)) * factor, lax.optimization_barrier(jnp.sum(middle_terms, axis=0)) * factor)
```

```python
import functools
import math

import jax
import jax.numpy as jnp
from jax import lax
from jax.experimental import pallas as pl
from jax.experimental.pallas import tpu as pltpu
from jax.sharding import PartitionSpec as P

SPAN = 2
CORES = 2
EPS = 1e-06
ROOT = math.sqrt(2.0 / math.pi)
CUBIC = 0.044715
CHUNK = 128
SUB = 16
MESH = pl.DeviceIdType.MESH
F32 = jnp.float32
BF16 = jnp.bfloat16


def tanh_part(u):
    u2 = u * u
    return u2, jnp.tanh(ROOT * u * (1.0 + CUBIC * u2))


def slope(u, u2, t):
    return 0.5 * (1.0 + t) + 0.5 * u * (1.0 - t * t) * (ROOT * (1.0 + 3.0 * CUBIC * u2))


def nt_dot(a, b):
    return lax.dot_general(a, b, (((1,), (1,)), ((), ())), preferred_element_type=F32)


def nn_dot(a, b):
    return jnp.dot(a, b, preferred_element_type=F32)


def kernel(
    n_seq, n_batch,
    lengths_hbm, act_hbm, ct_hbm, gain_in_hbm, tap_hbm, gain_mid_hbm, point_hbm,
    out_hbm, ing_hbm, gsum_in, gsum_mid,
    lengths, act, ct, gain_in, tap, gain_mid, point,
    hid, send_p, recv_p, cen, gmid, gc, recv_g, mid, gh, out, ing,
    acc_in, acc_mid, slots1, slots2,
    in_sem, act_sem, out_sem, ing_sem,
    p_send, p_recv, g_send, g_recv, r1_send, r1_recv, r2_send, r2_recv,
):
    rows, c = act.shape
    f = mid.shape[1]
    n = rows // CHUNK
    reach = SPAN * rows
    total = rows * n_seq
    seq = lax.axis_index("seq")
    batch = lax.axis_index("batch")
    core = lax.rem(seq, CORES)
    place = seq // CORES
    n_place = n_seq // CORES
    me1 = core * n_batch + batch
    n1 = CORES * n_batch

    def peer1(k):
        j = lax.rem(me1 + k, n1)
        return j, {"seq": seq - core + j // n_batch, "batch": lax.rem(j, n_batch)}

    def peer2(k):
        j = lax.rem(place + k, n_place)
        return j, {"seq": j * CORES + core, "batch": batch}

    barrier = pltpu.get_barrier_semaphore()
    for k in range(1, n_place):
        pl.semaphore_signal(barrier, inc=1, device_id=peer2(k)[1], device_id_type=MESH)
    for k in range(1, n1):
        pl.semaphore_signal(barrier, inc=1, device_id=peer1(k)[1], device_id_type=MESH)

    def part(i):
        return pl.ds(pl.multiple_of(i * CHUNK, CHUNK), CHUNK)

    def load_act(i):
        return pltpu.make_async_copy(act_hbm.at[0, part(i)], act.at[part(i)], act_sem.at[i])

    loads = [
        pltpu.make_async_copy(lengths_hbm, lengths, in_sem.at[0]),
        pltpu.make_async_copy(gain_in_hbm, gain_in, in_sem.at[1]),
        pltpu.make_async_copy(tap_hbm.at[0], tap.at[0], in_sem.at[2]),
        pltpu.make_async_copy(tap_hbm.at[2], tap.at[2], in_sem.at[3]),
        pltpu.make_async_copy(tap_hbm.at[1], tap.at[1], in_sem.at[4]),
        pltpu.make_async_copy(gain_mid_hbm, gain_mid, in_sem.at[5]),
        pltpu.make_async_copy(point_hbm, point, in_sem.at[6]),
        pltpu.make_async_copy(ct_hbm.at[0], ct, in_sem.at[7]),
    ]
    load_act(0).start()
    for k in (1, 2, 3):
        loads[k].start()
    for i in range(1, n):
        load_act(i).start()
    for k in (0, 4, 5, 6, 7):
        loads[k].start()

    ahead = {"seq": peer2(1)[1]["seq"]}
    behind = {"seq": peer2(n_place - 1)[1]["seq"]}

    def push(src, dst, send, recv, way, i):
        return pltpu.make_async_remote_copy(
            src_ref=src.at[part(i)],
            dst_ref=dst.at[way, part(i)],
            send_sem=send.at[way, i],
            recv_sem=recv.at[way, i],
            device_id=ahead if way == 0 else behind,
            device_id_type=MESH,
        )

    def push_p(way, i):
        return push(send_p.at[way], recv_p, p_send, p_recv, way, i)

    def push_g(way, i):
        return push(gc, recv_g, g_send, g_recv, way, i)

    def forward(i):
        load_act(i).wait()

        def norm(j, _):
            at = pl.ds(pl.multiple_of(i * CHUNK + j * SUB, SUB), SUB)
            v = act[at].astype(F32)
            r = lax.rsqrt(jnp.mean(v * v, axis=-1, keepdims=True) + EPS)
            u = v * r * gain_in[...]
            _, t = tanh_part(u)
            hid[at] = (0.5 * u * (1.0 + t)).astype(BF16)
            return 0

        lax.fori_loop(0, CHUNK // SUB, norm, 0)

    def products(i):
        send_p[0, part(i)] = nn_dot(hid[part(i)], tap[0]).astype(BF16)
        push_p(0, i).start()
        send_p[1, part(i)] = nn_dot(hid[part(i)], tap[2]).astype(BF16)
        push_p(1, i).start()

    loads[1].wait()
    forward(0)
    loads[2].wait()
    loads[3].wait()
    pl.semaphore_wait(barrier, n_place - 1 + n1 - 1)
    products(0)

    def first(i, _):
        forward(i)
        products(i)
        return 0

    lax.fori_loop(1, n, first, 0)

    for k in (0, 4, 5, 6, 7):
        loads[k].wait()
    acc_in[...] = jnp.zeros_like(acc_in)
    acc_mid[...] = jnp.zeros_like(acc_mid)

    def inner(i, _):
        cen[part(i)] = nn_dot(hid[part(i)], tap[1])
        gmid[part(i)] = nt_dot(ct[part(i)], point[...])
        return 0

    lax.fori_loop(0, n, inner, 0)

    bounds = []
    for k in range(lengths.shape[1]):
        bounds.append(lengths[0, k] + (bounds[-1] if bounds else 0))

    def owner(pos):
        return sum((pos >= b).astype(jnp.int32) for b in bounds)

    def valid(start, size):
        pos = seq * rows + start + lax.broadcasted_iota(jnp.int32, (size, 1), 0)
        own = owner(pos)
        before = jnp.where((pos >= reach) & (owner(pos - reach) == own), 1.0, 0.0)
        after = jnp.where((pos < total - reach) & (owner(pos + reach) == own), 1.0, 0.0)
        return before.astype(F32), after.astype(F32)

    def fold(x):
        return x[:8] + x[8:]

    def middle(i, _):
        push_p(0, i).wait_recv()
        push_p(1, i).wait_recv()

        def step(j, _):
            start = pl.multiple_of(i * CHUNK + j * SUB, SUB)
            at = pl.ds(start, SUB)
            before, after = valid(start, SUB)
            v = cen[at] + before * recv_p[0, at].astype(F32) + after * recv_p[1, at].astype(F32)
            r = lax.rsqrt(jnp.mean(v * v, axis=-1, keepdims=True) + EPS)
            nv = v * r
            u = nv * gain_mid[...]
            u2, t = tanh_part(u)
            mid[at] = (0.5 * u * (1.0 + t)).astype(BF16)
            du = gmid[at] * slope(u, u2, t)
            dun = du * nv
            acc_mid[...] += fold(dun)
            s = jnp.mean(dun * gain_mid[...], axis=-1, keepdims=True)
            gc[at] = (r * (du * gain_mid[...] - nv * s)).astype(BF16)
            return 0

        lax.fori_loop(0, CHUNK // SUB, step, 0)
        push_g(0, i).start()
        push_g(1, i).start()
        out[part(i)] = (
            act[part(i)].astype(F32) + nn_dot(mid[part(i)], point[...])
        ).astype(BF16)
        pltpu.make_async_copy(out.at[part(i)], out_hbm.at[0, part(i)], out_sem.at[i]).start()
        gh[part(i)] = nt_dot(gc[part(i)], tap[1])
        return 0

    lax.fori_loop(0, n, middle, 0)

    def backward(i, _):
        push_g(0, i).wait_recv()
        push_g(1, i).wait_recv()
        before, after = valid(pl.multiple_of(i * CHUNK, CHUNK), CHUNK)
        gb = (recv_g[0, part(i)].astype(F32) * before).astype(BF16)
        ga = (recv_g[1, part(i)].astype(F32) * after).astype(BF16)
        gh[part(i)] += nt_dot(gb, tap[2]) + nt_dot(ga, tap[0])

        def step(j, _):
            start = pl.multiple_of(i * CHUNK + j * SUB, SUB)
            at = pl.ds(start, SUB)
            v = act[at].astype(F32)
            r = lax.rsqrt(jnp.mean(v * v, axis=-1, keepdims=True) + EPS)
            nv = v * r
            u = nv * gain_in[...]
            u2, t = tanh_part(u)
            du = gh[at] * slope(u, u2, t)
            dun = du * nv
            acc_in[...] += fold(dun)
            s = jnp.mean(dun * gain_in[...], axis=-1, keepdims=True)
            dv = r * (du * gain_in[...] - nv * s)
            ing[at] = (ct[at].astype(F32) + dv).astype(BF16)
            return 0

        lax.fori_loop(0, CHUNK // SUB, step, 0)
        pltpu.make_async_copy(ing.at[part(i)], ing_hbm.at[0, part(i)], ing_sem.at[i]).start()
        return 0

    lax.fori_loop(0, n, backward, 0)

    def exchange(slots, me, peer, count, send, recv):
        def copy(k):
            j, device = peer(k)
            return pltpu.make_async_remote_copy(
                src_ref=slots.at[me],
                dst_ref=slots.at[me],
                send_sem=send.at[j],
                recv_sem=recv.at[me],
                device_id=device,
                device_id_type=MESH,
            )

        def arrival(k):
            j, device = peer(k)
            return pltpu.make_async_remote_copy(
                src_ref=slots.at[j],
                dst_ref=slots.at[j],
                send_sem=send.at[j],
                recv_sem=recv.at[j],
                device_id=device,
                device_id_type=MESH,
            )

        for k in range(1, count):
            copy(k).start()
        for k in range(1, count):
            arrival(k).wait_recv()
        summed = slots[0]
        for k in range(1, count):
            summed = summed + slots[k]
        return summed, copy

    slots1[me1, :, :c] = jnp.sum(acc_in[...], axis=0, keepdims=True)
    slots1[me1, :, c:] = jnp.sum(acc_mid[...], axis=0, keepdims=True)
    summed, copy1 = exchange(slots1, me1, peer1, n1, r1_send, r1_recv)
    slots2[place] = summed
    summed, copy2 = exchange(slots2, place, peer2, n_place, r2_send, r2_recv)
    summed = summed * (1.0 / math.sqrt(n_batch * total))
    gsum_in[...] = summed[:, :c]
    gsum_mid[...] = summed[:, c:]

    for k in range(1, n1):
        copy1(k).wait_send()
    for k in range(1, n_place):
        copy2(k).wait_send()
    for i in range(n):
        for way in range(2):
            push_p(way, i).wait_send()
            push_g(way, i).wait_send()
        pltpu.make_async_copy(out.at[part(i)], out_hbm.at[0, part(i)], out_sem.at[i]).wait()
        pltpu.make_async_copy(ing.at[part(i)], ing_hbm.at[0, part(i)], ing_sem.at[i]).wait()


def body(
    n_seq, n_batch,
    activations, cotangent, contig_lengths, gain_input, tap_weights, gain_middle, point_weights,
):
    _, rows, c = activations.shape
    f = tap_weights.shape[2]
    n = rows // CHUNK
    n1 = CORES * n_batch
    n2 = n_seq // CORES
    vmem = pltpu.VMEM
    dma = pltpu.SemaphoreType.DMA
    anywhere = pl.BlockSpec(memory_space=pl.ANY)
    whole = pl.BlockSpec(memory_space=vmem)
    result = pl.pallas_call(
        functools.partial(kernel, n_seq, n_batch),
        name="block",
        out_shape=[
            jax.ShapeDtypeStruct((1, rows, c), BF16),
            jax.ShapeDtypeStruct((1, rows, c), BF16),
            jax.ShapeDtypeStruct((1, c), F32),
            jax.ShapeDtypeStruct((1, f), F32),
        ],
        in_specs=[anywhere] * 7,
        out_specs=[anywhere, anywhere, whole, whole],
        scratch_shapes=[
            pltpu.SMEM(contig_lengths.shape, jnp.int32),
            vmem((rows, c), BF16),
            vmem((rows, c), BF16),
            vmem((1, c), F32),
            vmem((3, c, f), BF16),
            vmem((1, f), F32),
            vmem((f, c), BF16),
            vmem((rows, c), BF16),
            vmem((2, rows, f), BF16),
            vmem((2, rows, f), BF16),
            vmem((rows, f), F32),
            vmem((rows, f), F32),
            vmem((rows, f), BF16),
            vmem((2, rows, f), BF16),
            vmem((rows, f), BF16),
            vmem((rows, c), F32),
            vmem((rows, c), BF16),
            vmem((rows, c), BF16),
            vmem((8, c), F32),
            vmem((8, f), F32),
            vmem((n1, 1, c + f), F32),
            vmem((n2, 1, c + f), F32),
            dma((8,)),
            dma((n,)),
            dma((n,)),
            dma((n,)),
            dma((2, n)),
            dma((2, n)),
            dma((2, n)),
            dma((2, n)),
            dma((n1,)),
            dma((n1,)),
            dma((n2,)),
            dma((n2,)),
        ],
        compiler_params=pltpu.CompilerParams(
            collective_id=0, has_side_effects=True, vmem_limit_bytes=48 * 2**20
        ),
        cost_estimate=pl.CostEstimate(
            flops=16 * rows * c * f, bytes_accessed=16 * 2**20, transcendentals=3 * rows * c
        ),
    )(
        contig_lengths,
        activations,
        cotangent,
        gain_input.reshape(1, c),
        tap_weights,
        gain_middle.reshape(1, f),
        point_weights,
    )
    out, ing, gsum_in, gsum_mid = result
    return out, ing, gsum_in.reshape(c), gsum_mid.reshape(f)


def solution(mesh):
    placed = (
        P("batch", "seq", None),
        P("batch", "seq", None),
        P("batch", None),
        P(),
        P(),
        P(),
        P(),
    )
    return jax.shard_map(
        functools.partial(body, mesh.shape["seq"], mesh.shape["batch"]),
        mesh=mesh,
        in_specs=placed,
        out_specs=(P("batch", "seq", None), P("batch", "seq", None), P(), P()),
        check_vma=False,
    )
```

```python
import functools
import math

import jax
import jax.numpy as jnp
from jax import lax
from jax.experimental import pallas as pl
from jax.experimental.pallas import tpu as pltpu
from jax.sharding import PartitionSpec as P

SPAN = 2
CORES = 2
EPS = 1e-06
ROOT = math.sqrt(2.0 / math.pi)
CUBIC = 0.044715
SUB = 16
TILE = 256
GROUPS = ((0, 64, 1), (64, 64, 1), (128, 128, 2), (384, 64, 2))
RAW = 16
LANES = 128
MESH = pl.DeviceIdType.MESH
F32 = jnp.float32
BF16 = jnp.bfloat16
EXTENT = {"core": 2, "x": 4, "y": 4, "z": 8}
STAGES = (("core",), ("x", "y"), ("z",))
STAGE_SIZES = tuple(math.prod(EXTENT[a] for a in axes) for axes in STAGES)


def tanh_part(u):
    u2 = u * u
    return u2, jnp.tanh(ROOT * u * (1.0 + CUBIC * u2))


def slope(u, u2, t):
    return 0.5 * (1.0 + t) + 0.5 * u * (1.0 - t * t) * (ROOT * (1.0 + 3.0 * CUBIC * u2))


def nt_dot(a, b):
    return lax.dot_general(a, b, (((1,), (1,)), ((), ())), preferred_element_type=F32)


def nn_dot(a, b):
    return jnp.dot(a, b, preferred_element_type=F32)


def fold(x):
    return x[:8] + x[8:]


def kernel(
    n_seq, n_batch, n_contig,
    small, act_hbm, ct_hbm, tap_hbm, point_hbm,
    out_hbm, ing_hbm, gsum_in, gsum_mid,
    act, ct, tap, point, before, after,
    hid, raw, raw_hid, send_p, recv_p, cen, gmid, gc, recv_g, mid, gh, slp, inv, out, ing,
    gain_in_b, gain_mid_b, acc_in, acc_mid, packed, slots0, slots1, slots2,
    in_sem, act_sem, out_sem, ing_sem, raw_send, raw_recv,
    p_send, p_recv, g_send, g_recv,
    send0, send1, send2, got0, got1, got2,
):
    slots, ex_send, ex_got = (slots0, slots1, slots2), (send0, send1, send2), (got0, got1, got2)
    rows, c = act.shape
    f = mid.shape[1]
    reach = SPAN * rows
    total = rows * n_seq
    seq = lax.axis_index("seq")
    batch = lax.axis_index("batch")
    half_z = EXTENT["z"] // 2
    here = {
        "core": lax.rem(seq, CORES),
        "x": seq // (CORES * half_z),
        "y": lax.rem(batch, EXTENT["y"]),
        "z": lax.rem(seq // CORES, half_z) * 2 + batch // EXTENT["y"],
    }

    def device(at):
        return {
            "seq": (at["x"] * half_z + at["z"] // 2) * CORES + at["core"],
            "batch": lax.rem(at["z"], 2) * EXTENT["y"] + at["y"],
        }

    def group(axes):
        size = math.prod(EXTENT[a] for a in axes)
        me = 0
        for a in axes:
            me = me * EXTENT[a] + here[a]

        def peer(k):
            j = lax.rem(me + k, size)
            at, left = dict(here), j
            for a in reversed(axes):
                at[a] = lax.rem(left, EXTENT[a])
                left = left // EXTENT[a]
            return j, device(at)

        return size, me, peer

    ahead = {"seq": lax.rem(seq + SPAN, n_seq), "batch": batch}
    behind = {"seq": lax.rem(seq + n_seq - SPAN, n_seq), "batch": batch}
    stages = [group(axes) for axes in STAGES]

    def span(base, size, i):
        return pl.ds(pl.multiple_of(base + i * size, size), size)

    def load_act(k, at):
        return pltpu.make_async_copy(act_hbm.at[0, at], act.at[at], act_sem.at[k])

    load_tap = [pltpu.make_async_copy(tap_hbm.at[k], tap.at[k], in_sem.at[k]) for k in range(3)]
    load_point = pltpu.make_async_copy(point_hbm, point, in_sem.at[3])
    load_ct = pltpu.make_async_copy(ct_hbm.at[0], ct, in_sem.at[4])
    lead = GROUPS[0][1]
    load_first = load_act(0, pl.ds(0, lead))
    load_rest = load_act(1, pl.ds(lead, rows - lead))
    load_first.start()
    load_tap[0].start()
    load_tap[2].start()

    barrier = pltpu.get_barrier_semaphore()
    greeted = [ahead, behind]
    for size, _, peer in stages:
        greeted += [peer(k)[1] for k in range(1, size)]
    for d in greeted:
        pl.semaphore_signal(barrier, inc=1, device_id=d, device_id_type=MESH)

    def push(src, dst, send, recv, way, k, at):
        return pltpu.make_async_remote_copy(
            src_ref=src.at[at],
            dst_ref=dst.at[way, at],
            send_sem=send.at[way, k],
            recv_sem=recv.at[way, k],
            device_id=behind if way else ahead,
            device_id_type=MESH,
        )

    def push_p(way, k, at):
        return push(send_p.at[way], recv_p, p_send, p_recv, way, k, at)

    def push_g(way, k, at):
        return push(gc, recv_g, g_send, g_recv, way, k, at)

    def each_chunk(fn, groups=GROUPS, first=0):
        for base, size, count in groups:

            def one(i, _, base=base, size=size, first=first):
                fn(first + i, pl.multiple_of(base + i * size, size), size)
                return 0

            if count == 1:
                fn(first, base, size)
            else:
                lax.fori_loop(0, count, one, 0)
            first += count

    def each_sub(start, size, fn, unroll=2):
        def one(j, _):
            fn(pl.ds(pl.multiple_of(start + j * SUB, SUB), SUB), start + j * SUB)
            return 0

        lax.fori_loop(0, size // SUB, one, 0, unroll=unroll)

    def norm(at, _):
        v = act[at].astype(F32)
        r = lax.rsqrt(jnp.mean(v * v, axis=-1, keepdims=True) + EPS)
        u = v * r * gain_in_b[...]
        _, t = tanh_part(u)
        inv[at] = r
        hid[at] = (0.5 * u * (1.0 + t)).astype(BF16)

    def product(way, k, at):
        send_p[way, at] = nn_dot(hid[at], tap[2 * way]).astype(BF16)
        push_p(way, k, at).start()

    def push_raw(way):
        return pltpu.make_async_remote_copy(
            src_ref=act_hbm.at[0, pl.ds(0, RAW)],
            dst_ref=raw.at[way],
            send_sem=raw_send.at[way],
            recv_sem=raw_recv.at[way],
            device_id=behind if way else ahead,
            device_id_type=MESH,
        )

    def product_rows(k, start, size):
        return pl.ds(RAW, size - RAW) if isinstance(k, int) and k == 0 else pl.ds(start, size)

    gain_in_b[...] = jnp.broadcast_to(small[pl.ds(0, c)].reshape(1, c), (SUB, c))
    load_first.wait()
    each_sub(0, lead, norm)
    pl.semaphore_wait(barrier, len(greeted))
    push_raw(0).start()
    push_raw(1).start()
    load_tap[0].wait()
    product(0, 0, product_rows(0, 0, lead))
    load_tap[2].wait()
    product(1, 0, product_rows(0, 0, lead))
    load_rest.start()
    load_tap[1].start()
    load_point.start()
    load_ct.start()
    load_rest.wait()

    def forward(k, start, size):
        each_sub(start, size, norm)
        product(0, k, pl.ds(start, size))
        product(1, k, pl.ds(start, size))

    each_chunk(forward, GROUPS[1:], 1)

    load_tap[1].wait()
    load_point.wait()
    load_ct.wait()
    gain_mid_b[...] = jnp.broadcast_to(small[pl.ds(c, f)].reshape(1, f), (SUB, f))
    acc_in[...] = jnp.zeros_like(acc_in)
    acc_mid[...] = jnp.zeros_like(acc_mid)

    def tiles(width, fn):
        def one(i, _):
            fn(pl.ds(pl.multiple_of(i * TILE, TILE), TILE))
            return 0

        lax.fori_loop(0, width // TILE, one, 0)

    def inner(at):
        cen[:, at] = nn_dot(hid[...], tap[1, :, at])
        gmid[:, at] = nt_dot(ct[...], point[at])

    tiles(f, inner)

    lengths = small[pl.ds(c + f, LANES)].reshape(1, LANES)
    bounds = []
    for k in range(n_contig):
        bounds.append(lengths[:, k : k + 1] + (bounds[-1] if bounds else 0.0))

    def owner(pos):
        return sum((pos >= b).astype(F32) for b in bounds)

    def valid(at, row):
        pos = (seq * rows + row + lax.broadcasted_iota(jnp.int32, (SUB, 1), 0)).astype(F32)
        own = owner(pos)
        before[at] = jnp.where((pos >= reach) & (owner(pos - reach) == own), 1.0, 0.0)
        after[at] = jnp.where((pos < total - reach) & (owner(pos + reach) == own), 1.0, 0.0)

    each_sub(0, rows, valid)

    for way in range(2):
        push_raw(way).wait_recv()
        v = raw[way].astype(F32)
        u = v * lax.rsqrt(jnp.mean(v * v, axis=-1, keepdims=True) + EPS) * gain_in_b[...]
        raw_hid[...] = (0.5 * u * (1.0 + tanh_part(u)[1])).astype(BF16)
        recv_p[way, pl.ds(0, RAW)] = nn_dot(raw_hid[...], tap[2 * way]).astype(BF16)

    def exchange(slots, send, got, stage):
        count, me, peer = stage
        order = sorted(range(1, count), key=lambda k: -min(k, count - k))

        def copy(k, j, device_id):
            return pltpu.make_async_remote_copy(
                src_ref=slots.at[j],
                dst_ref=slots.at[j],
                send_sem=send.at[k],
                recv_sem=got.at[j],
                device_id=device_id,
                device_id_type=MESH,
            )

        def begin(value):
            slots[me] = value
            for k in order:
                copy(k, me, peer(k)[1]).start()

        def finish():
            for k in order:
                copy(k, *peer(k)).wait_recv()
            summed = slots[0]
            for k in range(1, count):
                summed = summed + slots[k]
            return summed

        def settle():
            for k in order:
                copy(k, me, peer(k)[1]).wait_send()

        return begin, finish, settle

    gain_stages = [exchange(*part) for part in zip(slots, ex_send, ex_got, stages)]
    scale = 1.0 / math.sqrt(n_batch * total)

    def middle(k, start, size):
        chunk = pl.ds(start, size)
        for way in range(2):
            push_p(way, k, product_rows(k, start, size)).wait_recv()

        def step(at, _):
            v = (
                cen[at]
                + before[at] * recv_p[0, at].astype(F32)
                + after[at] * recv_p[1, at].astype(F32)
            )
            r = lax.rsqrt(jnp.mean(v * v, axis=-1, keepdims=True) + EPS)
            nv = v * r
            u = nv * gain_mid_b[...]
            u2, t = tanh_part(u)
            mid[at] = (0.5 * u * (1.0 + t)).astype(BF16)
            du = gmid[at] * slope(u, u2, t)
            dun = du * nv
            acc_mid[...] += fold(dun)
            s = jnp.mean(dun * gain_mid_b[...], axis=-1, keepdims=True)
            gc[at] = (r * (du * gain_mid_b[...] - nv * s)).astype(BF16)

        each_sub(start, size, step)
        push_g(0, k, chunk).start()
        push_g(1, k, chunk).start()

    each_chunk(middle)

    def block(at):
        out[:, at] = (act[:, at].astype(F32) + nn_dot(mid[...], point[:, at])).astype(BF16)
        gh[:, at] = nt_dot(gc[...], tap[1, at])

    tiles(c, block)
    write_out = pltpu.make_async_copy(out, out_hbm.at[0], out_sem.at[0])
    write_out.start()

    def slopes(at, _):
        u = act[at].astype(F32) * inv[at] * gain_in_b[...]
        u2, t = tanh_part(u)
        slp[at] = slope(u, u2, t)

    each_sub(0, rows, slopes)

    def arrive(k, start, size):
        at = pl.ds(start, size)
        push_g(0, k, at).wait_recv()
        gb = (recv_g[0, at].astype(F32) * before[at]).astype(BF16)
        gh[at] += nt_dot(gb, tap[2])
        push_g(1, k, at).wait_recv()
        ga = (recv_g[1, at].astype(F32) * after[at]).astype(BF16)
        gh[at] += nt_dot(ga, tap[0])

    def terms(at, _):
        acc_in[...] += fold(gh[at] * slp[at] * (act[at].astype(F32) * inv[at]))

    def input_grad(at, _):
        r = inv[at]
        nv = act[at].astype(F32) * r
        dug = gh[at] * slp[at] * gain_in_b[...]
        s = jnp.mean(dug * nv, axis=-1, keepdims=True)
        ing[at] = (ct[at].astype(F32) + r * (dug - nv * s)).astype(BF16)

    def backward(k, start, size):
        arrive(k, start, size)
        each_sub(start, size, terms)
        each_sub(start, size, input_grad)

    base, size, count = GROUPS[-1]
    chunks = sum(g[2] for g in GROUPS)
    each_chunk(backward, GROUPS[:-1] + ((base, size, count - 1),))
    early = pl.ds(0, rows - size)
    late = pl.ds(rows - size, size)
    write_early = pltpu.make_async_copy(ing.at[early], ing_hbm.at[0, early], ing_sem.at[0])
    write_late = pltpu.make_async_copy(ing.at[late], ing_hbm.at[0, late], ing_sem.at[1])
    write_early.start()
    arrive(chunks - 1, rows - size, size)
    each_sub(rows - size, size, terms)

    lines = (c + f) // LANES
    for acc, base in ((acc_in, 0), (acc_mid, c // LANES)):
        line = jnp.sum(acc[...], axis=0, keepdims=True)
        for i in range(acc.shape[1] // LANES):
            packed[pl.ds(base + i, 1)] = line[:, i * LANES : (i + 1) * LANES]
    gain_stages[0][0](packed[...])
    gain_stages[1][0](gain_stages[0][1]())
    gain_stages[2][0](gain_stages[1][1]())
    each_sub(rows - size, size, input_grad)
    write_late.start()
    for stage in gain_stages[:2]:
        stage[2]()

    def sent(k, start, size):
        at = pl.ds(start, size)
        for way in range(2):
            push_p(way, k, product_rows(k, start, size)).wait_send()
            push_g(way, k, at).wait_send()

    each_chunk(sent)
    push_raw(0).wait_send()
    push_raw(1).wait_send()
    write_out.wait()
    write_early.wait()
    summed = gain_stages[2][1]() * scale
    for i in range(lines):
        to, j = (gsum_in, i) if i < c // LANES else (gsum_mid, i - c // LANES)
        to[pl.ds(j * LANES, LANES)] = summed[i]
    gain_stages[2][2]()
    write_late.wait()


def finish_kernel(out, ing, gsum_in, gsum_mid, out_to, ing_to, gsum_in_to, gsum_mid_to, sems):
    copies = [
        pltpu.make_async_copy(out, out_to, sems.at[0]),
        pltpu.make_async_copy(ing, ing_to, sems.at[1]),
    ]
    for copy in copies:
        copy.start()
    gsum_in_to[...] = gsum_in[...]
    gsum_mid_to[...] = gsum_mid[...]
    for copy in copies:
        copy.wait()


def body(
    n_seq, n_batch,
    activations, cotangent, contig_lengths, gain_input, tap_weights, gain_middle, point_weights,
):
    _, rows, c = activations.shape
    f = tap_weights.shape[2]
    n = sum(g[2] for g in GROUPS)
    vmem = pltpu.VMEM
    dma = pltpu.SemaphoreType.DMA
    anywhere = pl.BlockSpec(memory_space=pl.ANY)
    hbm = pl.BlockSpec(memory_space=pltpu.HBM)
    whole = pl.BlockSpec(memory_space=vmem)
    shapes = [
        jax.ShapeDtypeStruct((1, rows, c), BF16),
        jax.ShapeDtypeStruct((1, rows, c), BF16),
        jax.ShapeDtypeStruct((c,), F32),
        jax.ShapeDtypeStruct((f,), F32),
    ]
    lengths = jnp.pad(contig_lengths[0].astype(F32), (0, LANES - contig_lengths.shape[1]))
    small = jnp.concatenate([gain_input, gain_middle, lengths])
    result = pl.pallas_call(
        functools.partial(kernel, n_seq, n_batch, contig_lengths.shape[1]),
        name="block",
        out_shape=shapes,
        in_specs=[whole] + [hbm] * 4,
        out_specs=[anywhere, anywhere, whole, whole],
        scratch_shapes=[
            vmem((rows, c), BF16),
            vmem((rows, c), BF16),
            vmem((3, c, f), BF16),
            vmem((f, c), BF16),
            vmem((rows, 1), F32),
            vmem((rows, 1), F32),
            vmem((rows, c), BF16),
            vmem((2, RAW, c), BF16),
            vmem((RAW, c), BF16),
            vmem((2, rows, f), BF16),
            vmem((2, rows, f), BF16),
            vmem((rows, f), F32),
            vmem((rows, f), F32),
            vmem((rows, f), BF16),
            vmem((2, rows, f), BF16),
            vmem((rows, f), BF16),
            vmem((rows, c), F32),
            vmem((rows, c), F32),
            vmem((rows, 1), F32),
            vmem((rows, c), BF16),
            vmem((rows, c), BF16),
            vmem((SUB, c), F32),
            vmem((SUB, f), F32),
            vmem((8, c), F32),
            vmem((8, f), F32),
        ]
        + [vmem(((c + f) // LANES, LANES), F32)]
        + [vmem((size, (c + f) // LANES, LANES), F32) for size in STAGE_SIZES]
        + [dma((5,)), dma((2,)), dma((1,)), dma((2,)), dma((2,)), dma((2,))]
        + [dma((2, n))] * 4
        + [dma((size,)) for size in STAGE_SIZES] * 2,
        compiler_params=pltpu.CompilerParams(
            collective_id=0, has_side_effects=True, vmem_limit_bytes=50 * 2**20
        ),
        cost_estimate=pl.CostEstimate(
            flops=16 * rows * c * f, bytes_accessed=16 * 2**20, transcendentals=3 * rows * c
        ),
    )(
        small, activations, cotangent, tap_weights, point_weights
    )
    out, ing, gsum_in, gsum_mid = pl.pallas_call(
        finish_kernel,
        name="tail",
        out_shape=shapes,
        in_specs=[anywhere, anywhere, whole, whole],
        out_specs=[hbm, hbm, whole, whole],
        scratch_shapes=[dma((2,))],
        compiler_params=pltpu.CompilerParams(vmem_limit_bytes=8 * 2**20),
    )(*result)
    return out, ing, gsum_in, gsum_mid


def solution(mesh):
    placed = (
        P("batch", "seq", None),
        P("batch", "seq", None),
        P("batch", None),
        P(),
        P(),
        P(),
        P(),
    )
    return jax.shard_map(
        functools.partial(body, mesh.shape["seq"], mesh.shape["batch"]),
        mesh=mesh,
        in_specs=placed,
        out_specs=(P("batch", "seq", None), P("batch", "seq", None), P(), P()),
        check_vma=False,
    )
```

```python
import functools
import math

import jax
import jax.numpy as jnp
from jax import lax
from jax.experimental import pallas as pl
from jax.experimental.pallas import tpu as pltpu
from jax.sharding import PartitionSpec as P

SPAN = 2
CORES = 2
EPS = 1e-06
ROOT = math.sqrt(2.0 / math.pi)
CUBIC = 0.044715
SUB = 16
TILE = 256
GROUPS = ((0, 64, 1), (64, 64, 1), (128, 128, 3))
RAW = 16
LANES = 128
MESH = pl.DeviceIdType.MESH
F32 = jnp.float32
BF16 = jnp.bfloat16
EXTENT = {"core": 2, "x": 4, "y": 4, "z": 8}
STAGES = (("core",), ("x", "y"), ("z",))
STAGE_SIZES = tuple(math.prod(EXTENT[a] for a in axes) for axes in STAGES)


def tanh_part(u):
    u2 = u * u
    return u2, jnp.tanh(ROOT * u * (1.0 + CUBIC * u2))


def slope(u, u2, t):
    return 0.5 * (1.0 + t) + 0.5 * u * (1.0 - t * t) * (ROOT * (1.0 + 3.0 * CUBIC * u2))


def nt_dot(a, b):
    return lax.dot_general(a, b, (((1,), (1,)), ((), ())), preferred_element_type=F32)


def nn_dot(a, b):
    return jnp.dot(a, b, preferred_element_type=F32)


def fold(x):
    return x[:8] + x[8:]


def kernel(
    n_seq, n_batch, n_contig,
    small, act_hbm, ct_hbm, tap_hbm, point_hbm,
    out_hbm, ing_hbm, gsum_in, gsum_mid,
    act, ct, tap, tap_t, point, before, after,
    hid, raw, raw_hid, send_p, recv_p, cen, gmid, gc, recv_g, mid, gh, slp, inv, out, ing,
    gain_in_b, gain_mid_b, acc_in, acc_mid, packed, slots0, slots1, slots2,
    in_sem, act_sem, out_sem, ing_sem, raw_send, raw_recv,
    p_send, p_recv, g_send, g_recv,
    send0, send1, send2, got0, got1, got2,
):
    slots, ex_send, ex_got = (slots0, slots1, slots2), (send0, send1, send2), (got0, got1, got2)
    rows, c = act.shape
    f = mid.shape[1]
    reach = SPAN * rows
    total = rows * n_seq
    seq = lax.axis_index("seq")
    batch = lax.axis_index("batch")
    half_z = EXTENT["z"] // 2
    here = {
        "core": lax.rem(seq, CORES),
        "x": seq // (CORES * half_z),
        "y": lax.rem(batch, EXTENT["y"]),
        "z": lax.rem(seq // CORES, half_z) * 2 + batch // EXTENT["y"],
    }

    def device(at):
        return {
            "seq": (at["x"] * half_z + at["z"] // 2) * CORES + at["core"],
            "batch": lax.rem(at["z"], 2) * EXTENT["y"] + at["y"],
        }

    def group(axes):
        size = math.prod(EXTENT[a] for a in axes)
        me = 0
        for a in axes:
            me = me * EXTENT[a] + here[a]

        def peer(k):
            j = lax.rem(me + k, size)
            at, left = dict(here), j
            for a in reversed(axes):
                at[a] = lax.rem(left, EXTENT[a])
                left = left // EXTENT[a]
            return j, device(at)

        return size, me, peer

    ahead = {"seq": lax.rem(seq + SPAN, n_seq), "batch": batch}
    behind = {"seq": lax.rem(seq + n_seq - SPAN, n_seq), "batch": batch}
    stages = [group(axes) for axes in STAGES]

    def span(base, size, i):
        return pl.ds(pl.multiple_of(base + i * size, size), size)

    def load_act(k, at):
        return pltpu.make_async_copy(act_hbm.at[0, at], act.at[at], act_sem.at[k])

    load_tap = [pltpu.make_async_copy(tap_hbm.at[k], tap.at[k], in_sem.at[k]) for k in range(3)]
    load_point = pltpu.make_async_copy(point_hbm, point, in_sem.at[3])
    load_ct = pltpu.make_async_copy(ct_hbm.at[0], ct, in_sem.at[4])
    lead = GROUPS[0][1]
    load_first = load_act(0, pl.ds(0, lead))
    load_rest = load_act(1, pl.ds(lead, rows - lead))
    load_first.start()
    load_tap[0].start()
    load_tap[2].start()

    barrier = pltpu.get_barrier_semaphore()
    greeted = [ahead, behind]
    for size, _, peer in stages:
        greeted += [peer(k)[1] for k in range(1, size)]
    for d in greeted:
        pl.semaphore_signal(barrier, inc=1, device_id=d, device_id_type=MESH)

    def push(src, dst, send, recv, way, k, at):
        return pltpu.make_async_remote_copy(
            src_ref=src.at[at],
            dst_ref=dst.at[way, at],
            send_sem=send.at[way, k],
            recv_sem=recv.at[way, k],
            device_id=behind if way else ahead,
            device_id_type=MESH,
        )

    def push_p(way, k, at):
        return push(send_p.at[way], recv_p, p_send, p_recv, way, k, at)

    def push_g(way, k, at):
        return push(gc, recv_g, g_send, g_recv, way, k, at)

    def each_chunk(fn, groups=GROUPS, first=0):
        for base, size, count in groups:

            def one(i, _, base=base, size=size, first=first):
                fn(first + i, pl.multiple_of(base + i * size, size), size)
                return 0

            if count == 1:
                fn(first, base, size)
            else:
                lax.fori_loop(0, count, one, 0)
            first += count

    def each_sub(start, size, fn, unroll=2):
        def one(j, _):
            fn(pl.ds(pl.multiple_of(start + j * SUB, SUB), SUB), start + j * SUB)
            return 0

        lax.fori_loop(0, size // SUB, one, 0, unroll=unroll)

    def norm(at, _):
        v = act[at].astype(F32)
        r = lax.rsqrt(jnp.mean(v * v, axis=-1, keepdims=True) + EPS)
        u = v * r * gain_in_b[...]
        _, t = tanh_part(u)
        inv[at] = r
        hid[at] = (0.5 * u * (1.0 + t)).astype(BF16)

    def product(way, k, at):
        send_p[way, at] = nn_dot(hid[at], tap[2 * way]).astype(BF16)
        push_p(way, k, at).start()

    def push_raw(way):
        return pltpu.make_async_remote_copy(
            src_ref=act_hbm.at[0, pl.ds(0, RAW)],
            dst_ref=raw.at[way],
            send_sem=raw_send.at[way],
            recv_sem=raw_recv.at[way],
            device_id=behind if way else ahead,
            device_id_type=MESH,
        )

    def product_rows(k, start, size):
        return pl.ds(RAW, size - RAW) if isinstance(k, int) and k == 0 else pl.ds(start, size)

    gain_in_b[...] = jnp.broadcast_to(small[pl.ds(0, c)].reshape(1, c), (SUB, c))
    pl.semaphore_wait(barrier, len(greeted))
    push_raw(0).start()
    push_raw(1).start()
    load_first.wait()
    each_sub(0, lead, norm)
    load_tap[0].wait()
    product(0, 0, product_rows(0, 0, lead))
    load_tap[2].wait()
    product(1, 0, product_rows(0, 0, lead))
    load_rest.start()
    load_tap[1].start()
    load_point.start()
    load_ct.start()
    load_rest.wait()

    def forward(k, start, size):
        each_sub(start, size, norm)
        product(0, k, pl.ds(start, size))
        product(1, k, pl.ds(start, size))

    each_chunk(forward, GROUPS[1:], 1)

    load_tap[1].wait()
    load_point.wait()
    load_ct.wait()
    gain_mid_b[...] = jnp.broadcast_to(small[pl.ds(c, f)].reshape(1, f), (SUB, f))
    acc_in[...] = jnp.zeros_like(acc_in)
    acc_mid[...] = jnp.zeros_like(acc_mid)

    def tiles(width, fn):
        def one(i, _):
            fn(pl.ds(pl.multiple_of(i * TILE, TILE), TILE))
            return 0

        lax.fori_loop(0, width // TILE, one, 0)

    def inner(at):
        cen[:, at] = nn_dot(hid[...], tap[1, :, at])
        gmid[:, at] = nt_dot(ct[...], point[at])

    tiles(f, inner)

    lengths = small[pl.ds(c + f, LANES)].reshape(1, LANES)
    bounds = []
    for k in range(n_contig):
        bounds.append(lengths[:, k : k + 1] + (bounds[-1] if bounds else 0.0))

    def owner(pos):
        return sum((pos >= b).astype(F32) for b in bounds)

    def valid(at, row):
        pos = (seq * rows + row + lax.broadcasted_iota(jnp.int32, (SUB, 1), 0)).astype(F32)
        own = owner(pos)
        before[at] = jnp.where((pos >= reach) & (owner(pos - reach) == own), 1.0, 0.0)
        after[at] = jnp.where((pos < total - reach) & (owner(pos + reach) == own), 1.0, 0.0)

    each_sub(0, rows, valid)

    for way in range(2):
        push_raw(way).wait_recv()
        v = raw[way].astype(F32)
        u = v * lax.rsqrt(jnp.mean(v * v, axis=-1, keepdims=True) + EPS) * gain_in_b[...]
        raw_hid[...] = (0.5 * u * (1.0 + tanh_part(u)[1])).astype(BF16)
        recv_p[way, pl.ds(0, RAW)] = nn_dot(raw_hid[...], tap[2 * way]).astype(BF16)

    def exchange(slots, send, got, stage):
        count, me, peer = stage
        order = sorted(range(1, count), key=lambda k: -min(k, count - k))

        def copy(k, j, device_id):
            return pltpu.make_async_remote_copy(
                src_ref=slots.at[j],
                dst_ref=slots.at[j],
                send_sem=send.at[k],
                recv_sem=got.at[j],
                device_id=device_id,
                device_id_type=MESH,
            )

        def begin(value):
            slots[me] = value
            for k in order:
                copy(k, me, peer(k)[1]).start()

        def finish():
            for k in order:
                copy(k, *peer(k)).wait_recv()
            summed = slots[0]
            for k in range(1, count):
                summed = summed + slots[k]
            return summed

        def settle():
            for k in order:
                copy(k, me, peer(k)[1]).wait_send()

        return begin, finish, settle

    gain_stages = [exchange(*part) for part in zip(slots, ex_send, ex_got, stages)]
    scale = 1.0 / math.sqrt(n_batch * total)

    def middle(k, start, size):
        chunk = pl.ds(start, size)
        for way in range(2):
            push_p(way, k, product_rows(k, start, size)).wait_recv()

        def step(at, _):
            v = (
                cen[at]
                + before[at] * recv_p[0, at].astype(F32)
                + after[at] * recv_p[1, at].astype(F32)
            )
            r = lax.rsqrt(jnp.mean(v * v, axis=-1, keepdims=True) + EPS)
            nv = v * r
            u = nv * gain_mid_b[...]
            u2, t = tanh_part(u)
            mid[at] = (0.5 * u * (1.0 + t)).astype(BF16)
            du = gmid[at] * slope(u, u2, t)
            dun = du * nv
            acc_mid[...] += fold(dun)
            s = jnp.mean(dun * gain_mid_b[...], axis=-1, keepdims=True)
            gc[at] = (r * (du * gain_mid_b[...] - nv * s)).astype(BF16)

        each_sub(start, size, step)
        push_g(0, k, chunk).start()
        push_g(1, k, chunk).start()

    each_chunk(middle)

    def block(at):
        out[:, at] = (act[:, at].astype(F32) + nn_dot(mid[...], point[:, at])).astype(BF16)
        gh[:, at] = nt_dot(gc[...], tap[1, at])

    tiles(c, block)
    write_out = pltpu.make_async_copy(out, out_hbm.at[0], out_sem.at[0])
    write_out.start()

    def slopes(at, _):
        u = act[at].astype(F32) * inv[at] * gain_in_b[...]
        u2, t = tanh_part(u)
        slp[at] = slope(u, u2, t)

    each_sub(0, rows, slopes)

    def turn(at):
        for way in range(2):
            tap_t[way, :, at] = tap[2 * way, at].T

    tiles(c, turn)

    def arrive(k, start, size):
        at = pl.ds(start, size)
        push_g(0, k, at).wait_recv()
        gb = (recv_g[0, at].astype(F32) * before[at]).astype(BF16)
        gh[at] += nn_dot(gb, tap_t[1])
        push_g(1, k, at).wait_recv()
        ga = (recv_g[1, at].astype(F32) * after[at]).astype(BF16)
        gh[at] += nn_dot(ga, tap_t[0])

    def terms(at, _):
        acc_in[...] += fold(gh[at] * slp[at] * (act[at].astype(F32) * inv[at]))

    def input_grad(at, _):
        r = inv[at]
        nv = act[at].astype(F32) * r
        dug = gh[at] * slp[at] * gain_in_b[...]
        s = jnp.mean(dug * nv, axis=-1, keepdims=True)
        ing[at] = (ct[at].astype(F32) + r * (dug - nv * s)).astype(BF16)

    def backward(k, start, size):
        arrive(k, start, size)
        each_sub(start, size, terms)
        each_sub(start, size, input_grad)

    base, size, count = GROUPS[-1]
    chunks = sum(g[2] for g in GROUPS)
    each_chunk(backward, GROUPS[:-1] + ((base, size, count - 1),))
    early = pl.ds(0, rows - size)
    late = pl.ds(rows - size, size)
    write_early = pltpu.make_async_copy(ing.at[early], ing_hbm.at[0, early], ing_sem.at[0])
    write_late = pltpu.make_async_copy(ing.at[late], ing_hbm.at[0, late], ing_sem.at[1])
    write_early.start()
    arrive(chunks - 1, rows - size, size)
    each_sub(rows - size, size, terms)

    lines = (c + f) // LANES
    for acc, base in ((acc_in, 0), (acc_mid, c // LANES)):
        line = jnp.sum(acc[...], axis=0, keepdims=True)
        for i in range(acc.shape[1] // LANES):
            packed[pl.ds(base + i, 1)] = line[:, i * LANES : (i + 1) * LANES]
    gain_stages[0][0](packed[...])
    gain_stages[1][0](gain_stages[0][1]())
    gain_stages[2][0](gain_stages[1][1]())
    each_sub(rows - size, size, input_grad)
    write_late.start()
    for stage in gain_stages[:2]:
        stage[2]()

    def sent(k, start, size):
        at = pl.ds(start, size)
        for way in range(2):
            push_p(way, k, product_rows(k, start, size)).wait_send()
            push_g(way, k, at).wait_send()

    each_chunk(sent)
    push_raw(0).wait_send()
    push_raw(1).wait_send()
    write_out.wait()
    write_early.wait()
    summed = gain_stages[2][1]() * scale
    for i in range(lines):
        to, j = (gsum_in, i) if i < c // LANES else (gsum_mid, i - c // LANES)
        to[pl.ds(j * LANES, LANES)] = summed[i]
    gain_stages[2][2]()
    write_late.wait()


def finish_kernel(out, ing, gsum_in, gsum_mid, out_to, ing_to, gsum_in_to, gsum_mid_to, sems):
    copies = [
        pltpu.make_async_copy(out, out_to, sems.at[0]),
        pltpu.make_async_copy(ing, ing_to, sems.at[1]),
    ]
    for copy in copies:
        copy.start()
    gsum_in_to[...] = gsum_in[...]
    gsum_mid_to[...] = gsum_mid[...]
    for copy in copies:
        copy.wait()


def body(
    n_seq, n_batch,
    activations, cotangent, contig_lengths, gain_input, tap_weights, gain_middle, point_weights,
):
    _, rows, c = activations.shape
    f = tap_weights.shape[2]
    n = sum(g[2] for g in GROUPS)
    vmem = pltpu.VMEM
    dma = pltpu.SemaphoreType.DMA
    anywhere = pl.BlockSpec(memory_space=pl.ANY)
    hbm = pl.BlockSpec(memory_space=pltpu.HBM)
    whole = pl.BlockSpec(memory_space=vmem)
    shapes = [
        jax.ShapeDtypeStruct((1, rows, c), BF16),
        jax.ShapeDtypeStruct((1, rows, c), BF16),
        jax.ShapeDtypeStruct((c,), F32),
        jax.ShapeDtypeStruct((f,), F32),
    ]
    lengths = jnp.pad(contig_lengths[0].astype(F32), (0, LANES - contig_lengths.shape[1]))
    small = jnp.concatenate([gain_input, gain_middle, lengths])
    result = pl.pallas_call(
        functools.partial(kernel, n_seq, n_batch, contig_lengths.shape[1]),
        name="block",
        out_shape=shapes,
        in_specs=[whole] + [hbm] * 4,
        out_specs=[anywhere, anywhere, whole, whole],
        scratch_shapes=[
            vmem((rows, c), BF16),
            vmem((rows, c), BF16),
            vmem((3, c, f), BF16),
            vmem((2, f, c), BF16),
            vmem((f, c), BF16),
            vmem((rows, 1), F32),
            vmem((rows, 1), F32),
            vmem((rows, c), BF16),
            vmem((2, RAW, c), BF16),
            vmem((RAW, c), BF16),
            vmem((2, rows, f), BF16),
            vmem((2, rows, f), BF16),
            vmem((rows, f), F32),
            vmem((rows, f), F32),
            vmem((rows, f), BF16),
            vmem((2, rows, f), BF16),
            vmem((rows, f), BF16),
            vmem((rows, c), F32),
            vmem((rows, c), F32),
            vmem((rows, 1), F32),
            vmem((rows, c), BF16),
            vmem((rows, c), BF16),
            vmem((SUB, c), F32),
            vmem((SUB, f), F32),
            vmem((8, c), F32),
            vmem((8, f), F32),
        ]
        + [vmem(((c + f) // LANES, LANES), F32)]
        + [vmem((size, (c + f) // LANES, LANES), F32) for size in STAGE_SIZES]
        + [dma((5,)), dma((2,)), dma((1,)), dma((2,)), dma((2,)), dma((2,))]
        + [dma((2, n))] * 4
        + [dma((size,)) for size in STAGE_SIZES] * 2,
        compiler_params=pltpu.CompilerParams(
            collective_id=0, has_side_effects=True, vmem_limit_bytes=50 * 2**20
        ),
        cost_estimate=pl.CostEstimate(
            flops=16 * rows * c * f, bytes_accessed=16 * 2**20, transcendentals=3 * rows * c
        ),
    )(
        small, activations, cotangent, tap_weights, point_weights
    )
    out, ing, gsum_in, gsum_mid = pl.pallas_call(
        finish_kernel,
        name="tail",
        out_shape=shapes,
        in_specs=[anywhere, anywhere, whole, whole],
        out_specs=[hbm, hbm, whole, whole],
        scratch_shapes=[dma((2,))],
        compiler_params=pltpu.CompilerParams(vmem_limit_bytes=8 * 2**20),
    )(*result)
    return out, ing, gsum_in, gsum_mid


def solution(mesh):
    placed = (
        P("batch", "seq", None),
        P("batch", "seq", None),
        P("batch", None),
        P(),
        P(),
        P(),
        P(),
    )
    return jax.shard_map(
        functools.partial(body, mesh.shape["seq"], mesh.shape["batch"]),
        mesh=mesh,
        in_specs=placed,
        out_specs=(P("batch", "seq", None), P("batch", "seq", None), P(), P()),
        check_vma=False,
    )
```

```python
import functools
import math

import jax
import jax.numpy as jnp
from jax import lax
from jax.experimental import pallas as pl
from jax.experimental.pallas import tpu as pltpu
from jax.sharding import PartitionSpec as P

SPAN = 2
CORES = 2
EPS = 1e-06
ROOT = math.sqrt(2.0 / math.pi)
CUBIC = 0.044715
SUB = 16
TILE = 256
GROUPS = ((0, 64, 1), (64, 64, 1), (128, 128, 3))
RAW = 16
LANES = 128
MESH = pl.DeviceIdType.MESH
F32 = jnp.float32
BF16 = jnp.bfloat16
EXTENT = {"core": 2, "x": 4, "y": 4, "z": 8}
STAGES = (("core",), ("x", "y"), ("z",))
STAGE_SIZES = tuple(math.prod(EXTENT[a] for a in axes) for axes in STAGES)


def tanh_part(u):
    u2 = u * u
    return u2, jnp.tanh(ROOT * u * (1.0 + CUBIC * u2))


def slope(u, u2, t):
    return 0.5 * (1.0 + t) + 0.5 * u * (1.0 - t * t) * (ROOT * (1.0 + 3.0 * CUBIC * u2))


def nt_dot(a, b):
    return lax.dot_general(a, b, (((1,), (1,)), ((), ())), preferred_element_type=F32)


def nn_dot(a, b):
    return jnp.dot(a, b, preferred_element_type=F32)


def fold(x):
    return x[:8] + x[8:]


def kernel(
    n_seq, n_batch, n_contig,
    small, act_hbm, ct_hbm, tap_hbm, point_hbm,
    out_hbm, ing_hbm, gsum_in, gsum_mid,
    act, ct, tap, tap_t, point, before, after,
    hid, raw, raw_hid, send_p, recv_p, cen, gmid, gc, recv_g, mid, gh, slp, inv, out, ing,
    gain_in_b, gain_mid_b, acc_in, acc_mid, packed, slots0, slots1, slots2,
    in_sem, act_sem, out_sem, ing_sem, raw_send, raw_recv,
    p_send, p_recv, g_send, g_recv,
    send0, send1, send2, got0, got1, got2,
):
    slots, ex_send, ex_got = (slots0, slots1, slots2), (send0, send1, send2), (got0, got1, got2)
    rows, c = act.shape
    f = mid.shape[1]
    reach = SPAN * rows
    total = rows * n_seq
    seq = lax.axis_index("seq")
    batch = lax.axis_index("batch")
    half_z = EXTENT["z"] // 2
    here = {
        "core": lax.rem(seq, CORES),
        "x": seq // (CORES * half_z),
        "y": lax.rem(batch, EXTENT["y"]),
        "z": lax.rem(seq // CORES, half_z) * 2 + batch // EXTENT["y"],
    }

    def device(at):
        return {
            "seq": (at["x"] * half_z + at["z"] // 2) * CORES + at["core"],
            "batch": lax.rem(at["z"], 2) * EXTENT["y"] + at["y"],
        }

    def group(axes):
        size = math.prod(EXTENT[a] for a in axes)
        me = 0
        for a in axes:
            me = me * EXTENT[a] + here[a]

        def peer(k):
            j = lax.rem(me + k, size)
            at, left = dict(here), j
            for a in reversed(axes):
                at[a] = lax.rem(left, EXTENT[a])
                left = left // EXTENT[a]
            return j, device(at)

        return size, me, peer

    ahead = {"seq": lax.rem(seq + SPAN, n_seq), "batch": batch}
    behind = {"seq": lax.rem(seq + n_seq - SPAN, n_seq), "batch": batch}
    stages = [group(axes) for axes in STAGES]

    def span(base, size, i):
        return pl.ds(pl.multiple_of(base + i * size, size), size)

    def load_act(k, at):
        return pltpu.make_async_copy(act_hbm.at[0, at], act.at[at], act_sem.at[k])

    load_tap = [pltpu.make_async_copy(tap_hbm.at[k], tap.at[k], in_sem.at[k]) for k in range(3)]
    load_point = pltpu.make_async_copy(point_hbm, point, in_sem.at[3])
    load_ct = pltpu.make_async_copy(ct_hbm.at[0], ct, in_sem.at[4])
    lead = GROUPS[0][1]
    load_first = load_act(0, pl.ds(0, lead))
    load_rest = load_act(1, pl.ds(lead, rows - lead))
    load_first.start()
    load_tap[0].start()
    load_tap[2].start()

    barrier = pltpu.get_barrier_semaphore()
    greeted = [ahead, behind]
    for size, _, peer in stages:
        greeted += [peer(k)[1] for k in range(1, size)]
    for d in greeted:
        pl.semaphore_signal(barrier, inc=1, device_id=d, device_id_type=MESH)

    def push(src, dst, send, recv, way, k, at):
        return pltpu.make_async_remote_copy(
            src_ref=src.at[at],
            dst_ref=dst.at[way, at],
            send_sem=send.at[way, k],
            recv_sem=recv.at[way, k],
            device_id=behind if way else ahead,
            device_id_type=MESH,
        )

    def push_p(way, k, at):
        return push(send_p.at[way], recv_p, p_send, p_recv, way, k, at)

    def push_g(way, k, at):
        return push(gc, recv_g, g_send, g_recv, way, k, at)

    def each_chunk(fn, groups=GROUPS, first=0):
        for base, size, count in groups:

            def one(i, _, base=base, size=size, first=first):
                fn(first + i, pl.multiple_of(base + i * size, size), size)
                return 0

            if count == 1:
                fn(first, base, size)
            else:
                lax.fori_loop(0, count, one, 0)
            first += count

    def each_sub(start, size, fn, unroll=2):
        def one(j, _):
            fn(pl.ds(pl.multiple_of(start + j * SUB, SUB), SUB), start + j * SUB)
            return 0

        lax.fori_loop(0, size // SUB, one, 0, unroll=unroll)

    def norm(at, _):
        v = act[at].astype(F32)
        r = lax.rsqrt(jnp.mean(v * v, axis=-1, keepdims=True) + EPS)
        u = v * r * gain_in_b[...]
        _, t = tanh_part(u)
        inv[at] = r
        hid[at] = (0.5 * u * (1.0 + t)).astype(BF16)

    def product(way, k, at):
        send_p[way, at] = nn_dot(hid[at], tap[2 * way]).astype(BF16)
        push_p(way, k, at).start()

    def push_raw(way):
        return pltpu.make_async_remote_copy(
            src_ref=act_hbm.at[0, pl.ds(0, RAW)],
            dst_ref=raw.at[way],
            send_sem=raw_send.at[way],
            recv_sem=raw_recv.at[way],
            device_id=behind if way else ahead,
            device_id_type=MESH,
        )

    def product_rows(k, start, size):
        return pl.ds(RAW, size - RAW) if isinstance(k, int) and k == 0 else pl.ds(start, size)

    gain_in_b[...] = jnp.broadcast_to(small[pl.ds(0, c)].reshape(1, c), (SUB, c))
    pl.semaphore_wait(barrier, len(greeted))
    push_raw(0).start()
    push_raw(1).start()
    load_first.wait()
    each_sub(0, lead, norm)
    load_tap[0].wait()
    product(0, 0, product_rows(0, 0, lead))
    load_tap[2].wait()
    product(1, 0, product_rows(0, 0, lead))
    load_rest.start()
    load_tap[1].start()
    load_point.start()
    load_ct.start()
    load_rest.wait()

    def forward(k, start, size):
        each_sub(start, size, norm)
        product(0, k, pl.ds(start, size))
        product(1, k, pl.ds(start, size))

    each_chunk(forward, GROUPS[1:], 1)

    load_tap[1].wait()
    load_point.wait()
    load_ct.wait()
    gain_mid_b[...] = jnp.broadcast_to(small[pl.ds(c, f)].reshape(1, f), (SUB, f))
    acc_in[...] = jnp.zeros_like(acc_in)
    acc_mid[...] = jnp.zeros_like(acc_mid)

    def tiles(width, fn):
        def one(i, _):
            fn(pl.ds(pl.multiple_of(i * TILE, TILE), TILE))
            return 0

        lax.fori_loop(0, width // TILE, one, 0)

    def inner(at):
        cen[:, at] = nn_dot(hid[...], tap[1, :, at])
        gmid[:, at] = nt_dot(ct[...], point[at])

    tiles(f, inner)

    lengths = small[pl.ds(c + f, LANES)].reshape(1, LANES)
    bounds = []
    for k in range(n_contig):
        bounds.append(lengths[:, k : k + 1] + (bounds[-1] if bounds else 0.0))

    def owner(pos):
        return sum((pos >= b).astype(F32) for b in bounds)

    def valid(at, row):
        pos = (seq * rows + row + lax.broadcasted_iota(jnp.int32, (SUB, 1), 0)).astype(F32)
        own = owner(pos)
        before[at] = jnp.where((pos >= reach) & (owner(pos - reach) == own), 1.0, 0.0)
        after[at] = jnp.where((pos < total - reach) & (owner(pos + reach) == own), 1.0, 0.0)

    each_sub(0, rows, valid)

    for way in range(2):
        push_raw(way).wait_recv()
        v = raw[way].astype(F32)
        u = v * lax.rsqrt(jnp.mean(v * v, axis=-1, keepdims=True) + EPS) * gain_in_b[...]
        raw_hid[...] = (0.5 * u * (1.0 + tanh_part(u)[1])).astype(BF16)
        recv_p[way, pl.ds(0, RAW)] = nn_dot(raw_hid[...], tap[2 * way]).astype(BF16)

    def exchange(slots, send, got, stage):
        count, me, peer = stage
        order = sorted(range(1, count), key=lambda k: -min(k, count - k))

        def copy(k, j, device_id):
            return pltpu.make_async_remote_copy(
                src_ref=slots.at[j],
                dst_ref=slots.at[j],
                send_sem=send.at[k],
                recv_sem=got.at[j],
                device_id=device_id,
                device_id_type=MESH,
            )

        def begin(value):
            slots[me] = value
            for k in order:
                copy(k, me, peer(k)[1]).start()

        def finish():
            for k in order:
                copy(k, *peer(k)).wait_recv()
            summed = slots[0]
            for k in range(1, count):
                summed = summed + slots[k]
            return summed

        def settle():
            for k in order:
                copy(k, me, peer(k)[1]).wait_send()

        return begin, finish, settle

    gain_stages = [exchange(*part) for part in zip(slots, ex_send, ex_got, stages)]
    scale = 1.0 / math.sqrt(n_batch * total)

    def middle(k, start, size):
        chunk = pl.ds(start, size)
        for way in range(2):
            push_p(way, k, product_rows(k, start, size)).wait_recv()

        def step(at, _):
            v = (
                cen[at]
                + before[at] * recv_p[0, at].astype(F32)
                + after[at] * recv_p[1, at].astype(F32)
            )
            r = lax.rsqrt(jnp.mean(v * v, axis=-1, keepdims=True) + EPS)
            nv = v * r
            u = nv * gain_mid_b[...]
            u2, t = tanh_part(u)
            mid[at] = (0.5 * u * (1.0 + t)).astype(BF16)
            du = gmid[at] * slope(u, u2, t)
            dun = du * nv
            acc_mid[...] += fold(dun)
            s = jnp.mean(dun * gain_mid_b[...], axis=-1, keepdims=True)
            gc[at] = (r * (du * gain_mid_b[...] - nv * s)).astype(BF16)

        each_sub(start, size, step)
        push_g(0, k, chunk).start()
        push_g(1, k, chunk).start()

    each_chunk(middle)

    def block(at):
        out[:, at] = (act[:, at].astype(F32) + nn_dot(mid[...], point[:, at])).astype(BF16)
        gh[:, at] = nt_dot(gc[...], tap[1, at])

    tiles(c, block)
    write_out = pltpu.make_async_copy(out, out_hbm.at[0], out_sem.at[0])
    write_out.start()

    def slopes(at, _):
        u = act[at].astype(F32) * inv[at] * gain_in_b[...]
        u2, t = tanh_part(u)
        slp[at] = slope(u, u2, t)

    each_sub(0, rows, slopes)

    def turn(at):
        for way in range(2):
            tap_t[way, :, at] = tap[2 * way, at].T

    tiles(c, turn)

    def arrive(k, start, size):
        at = pl.ds(start, size)
        push_g(0, k, at).wait_recv()
        gb = (recv_g[0, at].astype(F32) * before[at]).astype(BF16)
        push_g(1, k, at).wait_recv()
        ga = (recv_g[1, at].astype(F32) * after[at]).astype(BF16)
        gh[at] += nn_dot(gb, tap_t[1]) + nn_dot(ga, tap_t[0])

    def terms(at, _):
        acc_in[...] += fold(gh[at] * slp[at] * (act[at].astype(F32) * inv[at]))

    def input_grad(at, _):
        r = inv[at]
        nv = act[at].astype(F32) * r
        dug = gh[at] * slp[at] * gain_in_b[...]
        s = jnp.mean(dug * nv, axis=-1, keepdims=True)
        ing[at] = (ct[at].astype(F32) + r * (dug - nv * s)).astype(BF16)

    def terms_and_grad(at, row):
        terms(at, row)
        input_grad(at, row)

    def backward(k, start, size):
        arrive(k, start, size)
        each_sub(start, size, terms_and_grad)

    base, size, count = GROUPS[-1]
    chunks = sum(g[2] for g in GROUPS)
    each_chunk(backward, GROUPS[:-1] + ((base, size, count - 1),))
    early = pl.ds(0, rows - size)
    late = pl.ds(rows - size, size)
    write_early = pltpu.make_async_copy(ing.at[early], ing_hbm.at[0, early], ing_sem.at[0])
    write_late = pltpu.make_async_copy(ing.at[late], ing_hbm.at[0, late], ing_sem.at[1])
    write_early.start()
    arrive(chunks - 1, rows - size, size)
    each_sub(rows - size, size, terms)

    lines = (c + f) // LANES
    for acc, base in ((acc_in, 0), (acc_mid, c // LANES)):
        line = jnp.sum(acc[...], axis=0, keepdims=True)
        for i in range(acc.shape[1] // LANES):
            packed[pl.ds(base + i, 1)] = line[:, i * LANES : (i + 1) * LANES]
    gain_stages[0][0](packed[...])
    gain_stages[1][0](gain_stages[0][1]())
    gain_stages[2][0](gain_stages[1][1]())
    each_sub(rows - size, size, input_grad)
    write_late.start()
    for stage in gain_stages[:2]:
        stage[2]()

    def sent(k, start, size):
        at = pl.ds(start, size)
        for way in range(2):
            push_p(way, k, product_rows(k, start, size)).wait_send()
            push_g(way, k, at).wait_send()

    each_chunk(sent)
    push_raw(0).wait_send()
    push_raw(1).wait_send()
    write_out.wait()
    write_early.wait()
    summed = gain_stages[2][1]() * scale
    for i in range(lines):
        to, j = (gsum_in, i) if i < c // LANES else (gsum_mid, i - c // LANES)
        to[pl.ds(j * LANES, LANES)] = summed[i]
    gain_stages[2][2]()
    write_late.wait()


def finish_kernel(out, ing, gsum_in, gsum_mid, out_to, ing_to, gsum_in_to, gsum_mid_to, sems):
    copies = [
        pltpu.make_async_copy(out, out_to, sems.at[0]),
        pltpu.make_async_copy(ing, ing_to, sems.at[1]),
    ]
    for copy in copies:
        copy.start()
    gsum_in_to[...] = gsum_in[...]
    gsum_mid_to[...] = gsum_mid[...]
    for copy in copies:
        copy.wait()


def body(
    n_seq, n_batch,
    activations, cotangent, contig_lengths, gain_input, tap_weights, gain_middle, point_weights,
):
    _, rows, c = activations.shape
    f = tap_weights.shape[2]
    n = sum(g[2] for g in GROUPS)
    vmem = pltpu.VMEM
    dma = pltpu.SemaphoreType.DMA
    anywhere = pl.BlockSpec(memory_space=pl.ANY)
    hbm = pl.BlockSpec(memory_space=pltpu.HBM)
    whole = pl.BlockSpec(memory_space=vmem)
    shapes = [
        jax.ShapeDtypeStruct((1, rows, c), BF16),
        jax.ShapeDtypeStruct((1, rows, c), BF16),
        jax.ShapeDtypeStruct((c,), F32),
        jax.ShapeDtypeStruct((f,), F32),
    ]
    lengths = jnp.pad(contig_lengths[0].astype(F32), (0, LANES - contig_lengths.shape[1]))
    small = jnp.concatenate([gain_input, gain_middle, lengths])
    result = pl.pallas_call(
        functools.partial(kernel, n_seq, n_batch, contig_lengths.shape[1]),
        name="block",
        out_shape=shapes,
        in_specs=[whole] + [hbm] * 4,
        out_specs=[anywhere, anywhere, whole, whole],
        scratch_shapes=[
            vmem((rows, c), BF16),
            vmem((rows, c), BF16),
            vmem((3, c, f), BF16),
            vmem((2, f, c), BF16),
            vmem((f, c), BF16),
            vmem((rows, 1), F32),
            vmem((rows, 1), F32),
            vmem((rows, c), BF16),
            vmem((2, RAW, c), BF16),
            vmem((RAW, c), BF16),
            vmem((2, rows, f), BF16),
            vmem((2, rows, f), BF16),
            vmem((rows, f), F32),
            vmem((rows, f), F32),
            vmem((rows, f), BF16),
            vmem((2, rows, f), BF16),
            vmem((rows, f), BF16),
            vmem((rows, c), F32),
            vmem((rows, c), F32),
            vmem((rows, 1), F32),
            vmem((rows, c), BF16),
            vmem((rows, c), BF16),
            vmem((SUB, c), F32),
            vmem((SUB, f), F32),
            vmem((8, c), F32),
            vmem((8, f), F32),
        ]
        + [vmem(((c + f) // LANES, LANES), F32)]
        + [vmem((size, (c + f) // LANES, LANES), F32) for size in STAGE_SIZES]
        + [dma((5,)), dma((2,)), dma((1,)), dma((2,)), dma((2,)), dma((2,))]
        + [dma((2, n))] * 4
        + [dma((size,)) for size in STAGE_SIZES] * 2,
        compiler_params=pltpu.CompilerParams(
            collective_id=0, has_side_effects=True, vmem_limit_bytes=50 * 2**20
        ),
        cost_estimate=pl.CostEstimate(
            flops=16 * rows * c * f, bytes_accessed=16 * 2**20, transcendentals=3 * rows * c
        ),
    )(
        small, activations, cotangent, tap_weights, point_weights
    )
    out, ing, gsum_in, gsum_mid = pl.pallas_call(
        finish_kernel,
        name="tail",
        out_shape=shapes,
        in_specs=[anywhere, anywhere, whole, whole],
        out_specs=[hbm, hbm, whole, whole],
        scratch_shapes=[dma((2,))],
        compiler_params=pltpu.CompilerParams(vmem_limit_bytes=8 * 2**20),
    )(*result)
    return out, ing, gsum_in, gsum_mid


def solution(mesh):
    placed = (
        P("batch", "seq", None),
        P("batch", "seq", None),
        P("batch", None),
        P(),
        P(),
        P(),
        P(),
    )
    return jax.shard_map(
        functools.partial(body, mesh.shape["seq"], mesh.shape["batch"]),
        mesh=mesh,
        in_specs=placed,
        out_specs=(P("batch", "seq", None), P("batch", "seq", None), P(), P()),
        check_vma=False,
    )
```
